32 devices in a mesh: tr: 4 (over z), tc: 8 (over y, x, core).
Axes of the slice: x: 2, y: 2, z: 4, core: 2. Of those that a mesh axis runs over, the one named last changes fastest.
Arguments:
- embeddings: bfloat16 [24576, 1024], P(('tr', 'tc')), may hold values from -100 to 100
- labels: int32 [24576], P(('tr', 'tc')), may hold values from 0 to 15, as said below
Outputs:
- best_sim: float32 [24576], P(('tr', 'tc'))
- weighted: float32 [24576], P(('tr', 'tc'))
- flag: float32 [24576], P(('tr', 'tc'))
The draws below stay inside these ranges and needn't reach their ends.
Inputs may be any that keep to these rules, and one draw needn't show every extreme that they name: In each aligned block of 768 files (one corpus shard), at most 576 files have labels // 4 equal to any one value g, and every shard has exactly 576 for some g; for every g and every c below 8, the shards c, c + 8, c + 16, ... together hold exactly 768 files with labels // 4 = g; every label is held by two or more files.
All inputs are finite; a program needn't handle non-finite values.
Results may differ from the reference program's by a relative error of at most 0.0013.
Values may be sent and summed in bfloat16 or wider, within the bound.
A program may use at most 128 MiB of HBM per device.

```python
import jax
import jax.numpy as jnp
from jax import lax

D = 1024
ROWS_DEV = 768
GROUP_CLUSTERS = 4
ROWS = 24576
N_TR = 4
N_TC = 8


def plan_labels(key):
    key = jax.random.fold_in(key, 7)
    key_wiggle, key_shift, key_perm, key_sub, key_other, key_offset = jax.random.split(key, 6)
    shards = N_TR * N_TC
    capacity = 3 * ROWS_DEV // N_TR
    remain = ROWS_DEV - capacity
    base = remain // (N_TR - 1)
    extra = remain - base * (N_TR - 1)
    wiggle = jax.random.randint(key_wiggle, (N_TC, N_TR - 1), 0, base // 2 + 1)
    others = base + wiggle - jnp.roll(wiggle, 1, axis=1) + (jnp.arange(N_TR - 1) < extra).astype(jnp.int32)[None, :]
    weights = jnp.concatenate([jnp.full((N_TC, 1), capacity, jnp.int32), others], axis=1)
    shift = jax.random.randint(key_shift, (N_TC,), 0, N_TR)
    row_ids = jnp.arange(N_TR)[:, None, None]
    col_ids = jnp.arange(N_TC)[None, :, None]
    target_ids = jnp.arange(N_TR)[None, None, :]
    which = (target_ids - row_ids - shift[None, :, None]) % N_TR
    counts = weights[jnp.broadcast_to(col_ids, which.shape), which].reshape(shards, N_TR)
    bounds = jnp.cumsum(counts, axis=1)
    positions = jnp.arange(ROWS_DEV)
    ordered = jnp.sum((positions[None, :, None] >= bounds[:, None, :]).astype(jnp.int32), axis=2)
    perm_keys = jax.random.split(key_perm, shards)
    owner = jax.vmap(lambda single, row: jax.random.permutation(single, row))(perm_keys, ordered)
    onehot = (owner[:, :, None] == jnp.arange(N_TR)[None, None, :]).astype(jnp.int32)
    running = jnp.sum(jnp.cumsum(onehot, axis=1) * onehot, axis=2)
    offset = jax.random.randint(key_offset, (N_TR,), 0, GROUP_CLUSTERS)
    first_pick = jax.random.randint(key_sub, (shards, ROWS_DEV), 0, GROUP_CLUSTERS)
    second_pick = jax.random.randint(key_other, (shards, ROWS_DEV), 0, GROUP_CLUSTERS)
    skewed = (jnp.minimum(first_pick, second_pick) + offset[owner]) % GROUP_CLUSTERS
    source = (jnp.arange(shards)[:, None] + offset[owner]) % GROUP_CLUSTERS
    member = jnp.where(running == 1, source, skewed)
    return (owner * GROUP_CLUSTERS + member).reshape(-1).astype(jnp.int32)


def draw_labels(key, part):
    return plan_labels(key)


def draw_embeddings(key, part):
    labels = plan_labels(key)
    key = jax.random.fold_in(key, 3)
    key_noise, key_center, key_mix, key_scale = jax.random.split(key, 4)
    centers = jnp.clip(jax.random.normal(key_center, (GROUP_CLUSTERS * N_TR, D), jnp.float32), -4.0, 4.0)
    noise = jnp.clip(jax.random.normal(key_noise, (ROWS, D), jnp.float32), -4.0, 4.0)
    mix = jax.random.uniform(key_mix, (GROUP_CLUSTERS * N_TR,), jnp.float32, 0.3, 0.8)
    scale = jnp.exp(jax.random.uniform(key_scale, (ROWS,), jnp.float32, -0.69, 2.08))
    drawn = noise + mix[labels][:, None] * centers[labels]
    return (drawn * scale[:, None]).astype(jnp.bfloat16)


def setup_inputs(seed: int = 0) -> dict:
    streams_of = jax.random.split(jax.random.key(seed), 3)
    embeddings = draw_embeddings(jax.random.fold_in(streams_of[2], 71), 0)
    labels = draw_labels(jax.random.fold_in(streams_of[2], 71), 0)
    return {"embeddings": embeddings, "labels": labels}


SCALE = 256.0
NEGATIVE = -1e+30
EPSILON = 1e-06
THRESHOLD = 0.3
SHARPNESS = 50.0

def reference(embeddings, labels):
    values = embeddings.astype(jnp.float32)
    unit = (values * lax.rsqrt(lax.optimization_barrier(jnp.sum(values * values, axis=1, keepdims=True)) + EPSILON)).astype(jnp.bfloat16)
    group = (labels // GROUP_CLUSTERS).astype(jnp.int32)
    order = jnp.argsort(group, stable=True).astype(jnp.int32)
    members = N_TC * ROWS_DEV
    sorted_unit = unit[order].reshape(N_TR, members, D)
    sorted_labels = labels[order].reshape(N_TR, members)
    member_index = jnp.arange(members, dtype=jnp.int32)

    def one_group(item):
        group_unit, group_labels = item

        def one_block(inner):
            block_unit, block_labels, block_index = inner
            sims = jnp.dot(block_unit, group_unit.T, preferred_element_type=jnp.float32)
            mask = (block_labels[:, None] == group_labels[None, :]) & (block_index[:, None] != member_index[None, :])
            scores = SCALE * sims
            top = lax.optimization_barrier(jnp.max(jnp.where(mask, scores, NEGATIVE), axis=1))
            terms = jnp.where(mask, jnp.exp(scores - top[:, None]), 0.0)
            return (top / SCALE, lax.optimization_barrier(jnp.sum(terms * sims, axis=1)) / lax.optimization_barrier(jnp.sum(terms, axis=1)))
        best, mean_sim = lax.map(one_block, (group_unit.reshape(N_TC, ROWS_DEV, D), group_labels.reshape(N_TC, ROWS_DEV), member_index.reshape(N_TC, ROWS_DEV)))
        return (best.reshape(-1), mean_sim.reshape(-1))
    best, mean_sim = lax.map(one_group, (sorted_unit, sorted_labels))
    best_sim = jnp.zeros((ROWS,), jnp.float32).at[order].set(best.reshape(-1))
    weighted = jnp.zeros((ROWS,), jnp.float32).at[order].set(mean_sim.reshape(-1))
    flag = jax.nn.sigmoid(SHARPNESS * (best_sim - THRESHOLD))
    return (best_sim, weighted, flag)
```

```python
import functools

import jax
import jax.numpy as jnp
from jax import lax
from jax.experimental import pallas as pl
from jax.experimental.pallas import tpu as pltpu
from jax.sharding import PartitionSpec as P

GROUP_CLUSTERS = 4


SCALE = 256.0
NEGATIVE = -1e30
EPSILON = 1e-06
THRESHOLD = 0.3
SHARPNESS = 50.0
TILE = 256
CHUNKS = 2


def stats_kernel(chunks, q_lo, q_hi, k_lo, k_hi, place, q_labels, k_labels, *refs):
    queries, keys = refs[:chunks], refs[chunks : 2 * chunks]
    best_ref, weighted_ref, sims_ref, top_ref = refs[2 * chunks :]
    block = pl.program_id(0)
    rows = queries[0].shape[0]
    tiles = rows // TILE

    @pl.when(block == 0)
    def _():
        top_ref[...] = jnp.full(top_ref.shape, NEGATIVE, jnp.float32)

    for kt in range(tiles):
        kn = block * tiles + kt
        for qt in range(tiles):
            own = block == place[0]
            q_rows = pl.ds(qt * TILE, TILE)
            k_rows = pl.ds(kt * TILE, TILE)

            @pl.when((q_lo[qt] <= k_hi[kn]) & (k_lo[kn] <= q_hi[qt]))
            def _():
                sims = None
                for c in range(chunks):
                    part = lax.dot_general(
                        queries[c][q_rows, :],
                        keys[c][k_rows, :],
                        (((1,), (1,)), ((), ())),
                        preferred_element_type=jnp.float32,
                    )
                    sims = part if sims is None else sims + part
                mask = q_labels[q_rows, :] == k_labels[0, :, k_rows]
                if qt == kt:
                    row = lax.broadcasted_iota(jnp.int32, (TILE, TILE), 0)
                    col = lax.broadcasted_iota(jnp.int32, (TILE, TILE), 1)
                    mask = mask & ((row != col) | jnp.logical_not(own))
                sims = jnp.where(mask, sims, NEGATIVE)
                sims_ref[kn, q_rows, :] = sims
                part = jnp.maximum(sims[:, :128], sims[:, 128:])
                top_ref[q_rows, :] = jnp.maximum(top_ref[q_rows, :], part)

    @pl.when(block == pl.num_programs(0) - 1)
    def _():
        for qt in range(tiles):
            q_rows = pl.ds(qt * TILE, TILE)
            best = jnp.max(top_ref[q_rows, :], axis=1, keepdims=True)

            def step(kn, carry):
                def visit(carry):
                    total, weight = carry
                    sims = sims_ref[kn, q_rows, :]
                    terms = jnp.exp(SCALE * (sims - best))
                    both = terms * sims
                    return (
                        total + (terms[:, :128] + terms[:, 128:]),
                        weight + (both[:, :128] + both[:, 128:]),
                    )

                meets = (q_lo[qt] <= k_hi[kn]) & (k_lo[kn] <= q_hi[qt])
                return lax.cond(meets, visit, lambda same: same, carry)

            zero = jnp.zeros((TILE, 128), jnp.float32)
            total, weight = lax.fori_loop(0, sims_ref.shape[0], step, (zero, zero))
            best_ref[q_rows, :] = best
            weighted_ref[q_rows, :] = jnp.sum(weight, axis=1, keepdims=True) / jnp.sum(
                total, axis=1, keepdims=True
            )


def cluster_stats(queries, keys, query_labels, key_labels, place):
    chunks = len(queries)
    rows, width = queries[0].shape
    members = keys[0].shape[0]
    q_tiles = query_labels.reshape(-1, TILE)
    k_tiles = key_labels.reshape(-1, TILE)
    smem = pl.BlockSpec(memory_space=pltpu.SMEM)
    scratch = rows * members * 4
    best, weighted = pl.pallas_call(
        functools.partial(stats_kernel, chunks),
        grid=(members // rows,),
        in_specs=[smem] * 5
        + [
            pl.BlockSpec((rows, 1), lambda b: (0, 0)),
            pl.BlockSpec((1, 1, rows), lambda b: (b, 0, 0)),
        ]
        + [pl.BlockSpec((rows, width), lambda b: (0, 0))] * chunks
        + [pl.BlockSpec((rows, width), lambda b: (b, 0))] * chunks,
        out_specs=[pl.BlockSpec((rows, 1), lambda b: (0, 0))] * 2,
        out_shape=[jax.ShapeDtypeStruct((rows, 1), jnp.float32)] * 2,
        scratch_shapes=[
            pltpu.VMEM((members // TILE, rows, TILE), jnp.float32),
            pltpu.VMEM((rows, 128), jnp.float32),
        ],
        compiler_params=pltpu.CompilerParams(vmem_limit_bytes=scratch + (16 << 20)),
        cost_estimate=pl.CostEstimate(
            flops=2 * rows * members * width * chunks,
            bytes_accessed=2 * members * width * chunks,
            transcendentals=rows * members,
        ),
    )(
        q_tiles[:, 0],
        q_tiles[:, -1],
        k_tiles[:, 0],
        k_tiles[:, -1],
        place.reshape(1),
        query_labels[:, None],
        key_labels.reshape(-1, 1, rows),
        *queries,
        *keys,
    )
    return best[:, 0], weighted[:, 0]


def permute(target, count, parts):
    matrix = (jnp.arange(count, dtype=jnp.int32)[:, None] == target[None, :]).astype(jnp.bfloat16)
    return [
        jnp.dot(matrix, part, preferred_element_type=jnp.float32).astype(jnp.bfloat16)
        for part in parts
    ]


def exclusive(values, axis):
    return jnp.cumsum(values, axis=axis) - values


def per_device(embeddings, labels):
    shard_rows, feature_dim = embeddings.shape
    tile_rows = lax.axis_size("tr")
    columns = lax.axis_size("tc")
    me = lax.axis_index("tr")
    place = lax.axis_index("tc")
    clusters = tile_rows * GROUP_CLUSTERS
    share = shard_rows // tile_rows
    capacity = -(-(share + tile_rows - 1) // 16) * 16
    i32 = jnp.int32

    onehot = labels[:, None] == jnp.arange(clusters, dtype=i32)[None, :]
    held = jnp.sum(onehot.astype(i32), axis=0)
    every = lax.all_gather(held, ("tr", "tc"), axis=0, tiled=False)
    every = every.reshape(tile_rows, columns, clusters)
    column = lax.dynamic_index_in_dim(every, place, 1, keepdims=False)

    index = jnp.arange(shard_rows, dtype=i32)
    lower = (index[:, None] > index[None, :]).astype(jnp.bfloat16)
    ahead = jnp.dot(lower, onehot.astype(jnp.bfloat16), preferred_element_type=jnp.float32)
    rank = jnp.sum(jnp.where(onehot, ahead, 0.0), axis=1).astype(i32)
    starts = exclusive(held, 0)
    order = jnp.sum(jnp.where(onehot, starts[None, :], 0), axis=1) + rank

    values = embeddings.astype(jnp.float32)
    unit = (values * lax.rsqrt(jnp.sum(values * values, axis=1, keepdims=True) + EPSILON)).astype(
        jnp.bfloat16
    )
    width = feature_dim // CHUNKS
    parts = [unit[:, c * width : (c + 1) * width] for c in range(CHUNKS)]

    def exchange(part, count):
        return lax.all_to_all(
            part.reshape(tile_rows, count, width), "tr", split_axis=0, concat_axis=0, tiled=True
        ).reshape(tile_rows * count, width)

    spread = permute(order % tile_rows * share + order // tile_rows, shard_rows, parts)
    spread = [exchange(part, share) for part in spread]

    local = exclusive(column, 1)
    group_count = column.reshape(tile_rows, tile_rows, GROUP_CLUSTERS).sum(2)
    group_start = exclusive(group_count, 1)
    via = jnp.arange(tile_rows, dtype=i32)

    def before(limit):
        return (limit[..., None] - via + tile_rows - 1) // tile_rows

    first = before(group_start)
    passed = before(group_start + group_count) - first
    base = exclusive(passed, 0) - first

    number = jnp.arange(share, dtype=i32)[None, :] * tile_rows + me
    inside = (number[:, :, None] >= group_start[:, None, :]) & (
        number[:, :, None] < (group_start + group_count)[:, None, :]
    )
    my_base = lax.dynamic_index_in_dim(base, me, 2, keepdims=False)
    lane = my_base[:, None, :] + number[:, :, None] // tile_rows
    target = jnp.sum(jnp.where(inside, via * capacity + lane, 0), axis=2).reshape(-1)
    routed = permute(target, tile_rows * capacity, spread)
    routed = [exchange(part, capacity) for part in routed]

    mine = lax.dynamic_slice_in_dim(column, me * GROUP_CLUSTERS, GROUP_CLUSTERS, 1)
    lengths = mine.T.reshape(-1)
    seg_start = exclusive(lengths, 0)
    seg_local = lax.dynamic_slice_in_dim(local, me * GROUP_CLUSTERS, GROUP_CLUSTERS, 1).T.reshape(-1)
    within = (index[:, None] >= seg_start[None, :]) & (
        index[:, None] < (seg_start + lengths)[None, :]
    )
    number = index + jnp.sum(jnp.where(within, (seg_local - seg_start)[None, :], 0), axis=1)
    route = number % tile_rows
    tables = lax.dynamic_index_in_dim(base, me, 1, keepdims=False)
    tables = jnp.tile(tables, (GROUP_CLUSTERS, 1))
    picked = jnp.sum(jnp.where(within[:, :, None], tables[None], 0), axis=1)
    offset = jnp.sum(jnp.where(route[:, None] == via[None, :], picked, 0), axis=1)
    source = route * capacity + offset + number // tile_rows
    matrix = (
        source[:, None] == jnp.arange(tile_rows * capacity, dtype=i32)[None, :]
    ).astype(jnp.bfloat16)
    queries = [
        jnp.dot(matrix, part, preferred_element_type=jnp.float32).astype(jnp.bfloat16)
        for part in routed
    ]
    keys = [lax.all_gather(part, "tc", axis=0, tiled=True) for part in queries]

    totals = lax.dynamic_slice_in_dim(every.sum(0), me * GROUP_CLUSTERS, GROUP_CLUSTERS, 1)
    ends = jnp.cumsum(totals, axis=1)[:, : GROUP_CLUSTERS - 1]
    key_labels = jnp.sum((index[None, :, None] >= ends[:, None, :]).astype(i32), axis=2)
    query_labels = lax.dynamic_index_in_dim(key_labels, place, 0, keepdims=False)

    best, weighted = cluster_stats(queries, keys, query_labels, key_labels.reshape(-1), place)

    back = lax.all_gather(jnp.stack([best, weighted]), "tr", axis=1, tiled=True)
    shard_before = exclusive(column, 0)
    begin = exclusive(column.sum(0), 0) + lax.dynamic_index_in_dim(
        shard_before, me, 0, keepdims=False
    )
    position = jnp.sum(jnp.where(onehot, begin[None, :], 0), axis=1) + rank
    here = position[:, None] == jnp.arange(tile_rows * shard_rows, dtype=i32)[None, :]
    best_sim = jnp.sum(jnp.where(here, back[0][None, :], 0.0), axis=1)
    mean_sim = jnp.sum(jnp.where(here, back[1][None, :], 0.0), axis=1)
    flag = jax.nn.sigmoid(SHARPNESS * (best_sim - THRESHOLD))
    return (best_sim, mean_sim, flag)


def solution(mesh):
    placed = (P(("tr", "tc"), None), P(("tr", "tc")))
    return jax.shard_map(
        per_device,
        mesh=mesh,
        in_specs=placed,
        out_specs=(P(("tr", "tc")), P(("tr", "tc")), P(("tr", "tc"))),
        check_vma=False,
    )
```

```python
import functools

import jax
import jax.numpy as jnp
from jax import lax
from jax.experimental import pallas as pl
from jax.experimental.pallas import tpu as pltpu
from jax.sharding import PartitionSpec as P

GROUP_CLUSTERS = 4


SCALE = 256.0
NEGATIVE = -1e30
EPSILON = 1e-06
THRESHOLD = 0.3
SHARPNESS = 50.0
TILE = 256
CHUNKS = 1
MESH = pl.DeviceIdType.MESH


def stats_kernel(chunks, q_lo, q_hi, k_lo, k_hi, place, q_labels, k_labels, *refs):
    queries, keys = refs[:chunks], refs[chunks : 2 * chunks]
    best_ref, weighted_ref, sims_ref, top_ref = refs[2 * chunks :]
    block = pl.program_id(0)
    rows = queries[0].shape[0]
    tiles = rows // TILE

    @pl.when(block == 0)
    def _():
        top_ref[...] = jnp.full(top_ref.shape, NEGATIVE, jnp.float32)

    for kt in range(tiles):
        kn = block * tiles + kt
        for qt in range(tiles):
            own = block == place[0]
            q_rows = pl.ds(qt * TILE, TILE)
            k_rows = pl.ds(kt * TILE, TILE)

            @pl.when((q_lo[qt] <= k_hi[kn]) & (k_lo[kn] <= q_hi[qt]))
            def _():
                sims = None
                for c in range(chunks):
                    part = lax.dot_general(
                        queries[c][q_rows, :],
                        keys[c][k_rows, :],
                        (((1,), (1,)), ((), ())),
                        preferred_element_type=jnp.float32,
                    )
                    sims = part if sims is None else sims + part
                mask = q_labels[q_rows, :] == k_labels[0, :, k_rows]
                if qt == kt:
                    row = lax.broadcasted_iota(jnp.int32, (TILE, TILE), 0)
                    col = lax.broadcasted_iota(jnp.int32, (TILE, TILE), 1)
                    mask = mask & ((row != col) | jnp.logical_not(own))
                sims = jnp.where(mask, sims, NEGATIVE)
                sims_ref[kn, q_rows, :] = sims
                part = jnp.maximum(sims[:, :128], sims[:, 128:])
                top_ref[q_rows, :] = jnp.maximum(top_ref[q_rows, :], part)

    @pl.when(block == pl.num_programs(0) - 1)
    def _():
        for qt in range(tiles):
            q_rows = pl.ds(qt * TILE, TILE)
            best = jnp.max(top_ref[q_rows, :], axis=1, keepdims=True)

            def step(kn, carry):
                def visit(carry):
                    total, weight = carry
                    sims = sims_ref[kn, q_rows, :]
                    terms = jnp.exp(SCALE * (sims - best))
                    both = terms * sims
                    return (
                        total + (terms[:, :128] + terms[:, 128:]),
                        weight + (both[:, :128] + both[:, 128:]),
                    )

                meets = (q_lo[qt] <= k_hi[kn]) & (k_lo[kn] <= q_hi[qt])
                return lax.cond(meets, visit, lambda same: same, carry)

            zero = jnp.zeros((TILE, 128), jnp.float32)
            total, weight = lax.fori_loop(0, sims_ref.shape[0], step, (zero, zero))
            best_ref[q_rows, :] = best
            weighted_ref[q_rows, :] = jnp.sum(weight, axis=1, keepdims=True) / jnp.sum(
                total, axis=1, keepdims=True
            )


def cluster_stats(queries, keys, query_labels, key_labels, place):
    chunks = len(queries)
    rows, width = queries[0].shape
    members = keys[0].shape[0]
    q_tiles = query_labels.reshape(-1, TILE)
    k_tiles = key_labels.reshape(-1, TILE)
    smem = pl.BlockSpec(memory_space=pltpu.SMEM)
    scratch = rows * members * 4
    best, weighted = pl.pallas_call(
        functools.partial(stats_kernel, chunks),
        grid=(members // rows,),
        in_specs=[smem] * 5
        + [
            pl.BlockSpec((rows, 1), lambda b: (0, 0)),
            pl.BlockSpec((1, 1, rows), lambda b: (b, 0, 0)),
        ]
        + [pl.BlockSpec((rows, width), lambda b: (0, 0))] * chunks
        + [pl.BlockSpec((rows, width), lambda b: (b, 0))] * chunks,
        out_specs=[pl.BlockSpec((rows, 1), lambda b: (0, 0))] * 2,
        out_shape=[jax.ShapeDtypeStruct((rows, 1), jnp.float32)] * 2,
        scratch_shapes=[
            pltpu.VMEM((members // TILE, rows, TILE), jnp.float32),
            pltpu.VMEM((rows, 128), jnp.float32),
        ],
        compiler_params=pltpu.CompilerParams(vmem_limit_bytes=scratch + (16 << 20)),
        cost_estimate=pl.CostEstimate(
            flops=2 * rows * members * width * chunks,
            bytes_accessed=2 * members * width * chunks,
            transcendentals=rows * members,
        ),
    )(
        q_tiles[:, 0],
        q_tiles[:, -1],
        k_tiles[:, 0],
        k_tiles[:, -1],
        place.reshape(1),
        query_labels[:, None],
        key_labels.reshape(-1, 1, rows),
        *queries,
        *keys,
    )
    return best[:, 0], weighted[:, 0]


def count_kernel(rows, columns, held, column, totals, mine, sems):
    me, place = lax.axis_index("tr"), lax.axis_index("tc")
    tr_peers = [lax.rem(me + d, rows) for d in range(1, rows)]
    tc_peers = [lax.rem(place + d, columns) for d in range(1, columns)]
    barrier = pltpu.get_barrier_semaphore()
    for peer in tr_peers:
        pl.semaphore_signal(barrier, inc=1, device_id=(peer, place), device_id_type=MESH)
    for peer in tc_peers:
        pl.semaphore_signal(barrier, inc=1, device_id=(me, peer), device_id_type=MESH)
    pl.semaphore_wait(barrier, rows + columns - 2)

    def exchange(source, buffer, index, peers, first, whom):
        copies = []
        for d, peer in enumerate(peers):
            copy = pltpu.make_async_remote_copy(
                src_ref=source,
                dst_ref=buffer.at[index],
                send_sem=sems.at[0, first + d],
                recv_sem=sems.at[1, first + d],
                device_id=whom(peer),
                device_id_type=MESH,
            )
            copy.start()
            copies.append(copy)
        buffer[index] = source[...]
        for copy in copies:
            copy.wait()

    exchange(held, column, me, tr_peers, 0, lambda peer: (peer, place))
    mine[...] = jnp.sum(column[...], axis=0)
    exchange(mine, totals, place, tc_peers, rows - 1, lambda peer: (me, peer))


def gather_counts(held, rows, columns):
    clusters = held.shape[0]
    padded = jnp.zeros((8, 128), jnp.int32).at[0, :clusters].set(held)
    vmem = pl.BlockSpec(memory_space=pltpu.VMEM)
    column, totals = pl.pallas_call(
        functools.partial(count_kernel, rows, columns),
        in_specs=[vmem],
        out_specs=[vmem, vmem],
        out_shape=[
            jax.ShapeDtypeStruct((rows, 8, 128), jnp.int32),
            jax.ShapeDtypeStruct((columns, 8, 128), jnp.int32),
        ],
        scratch_shapes=[
            pltpu.VMEM((8, 128), jnp.int32),
            pltpu.SemaphoreType.DMA((2, rows + columns - 2)),
        ],
        compiler_params=pltpu.CompilerParams(collective_id=0, has_side_effects=True),
    )(padded)
    return column[:, 0, :clusters], totals[:, 0, :clusters]


def plane_kernel(tile_rows, q_labels, k_labels, own, back, blocks, stats, part, theirs, sems):
    me, place = lax.axis_index("tr"), lax.axis_index("tc")
    sibling = place + 1 - 2 * (place % 2)
    across = place + 2 - 4 * ((place // 2) % 2)
    along = place + 4 - 8 * (place // 4)
    rows = own.shape[0]
    tiles = rows // TILE
    peers = [(me, sibling), (me, across), (me, along)]
    peers += [(lax.rem(me + d, tile_rows), place) for d in range(1, tile_rows)]
    barrier = pltpu.get_barrier_semaphore()
    for peer in peers:
        pl.semaphore_signal(barrier, inc=1, device_id=peer, device_id_type=MESH)
    pl.semaphore_wait(barrier, len(peers))

    def send(source, target, number, peer):
        copy = pltpu.make_async_remote_copy(
            src_ref=source,
            dst_ref=target,
            send_sem=sems.at[0, number],
            recv_sem=sems.at[1, number],
            device_id=peer,
            device_id_type=MESH,
        )
        copy.start()
        return copy

    def cut(c):
        return pl.ds(c * TILE, TILE)

    direct, passed = [], []
    for c in range(tiles):
        direct.append(
            [
                send(own.at[cut(c), :], blocks.at[2, cut(c), :], 4 * c, peers[1]),
                send(own.at[cut(c), :], blocks.at[3, cut(c), :], 4 * c + 1, peers[2]),
            ]
        )
    from_sibling = send(own, blocks.at[1], 4 * tiles, peers[0])
    blocks[0] = own[...]
    for side in range(2):
        stats[side, 0] = jnp.full((rows, 128), NEGATIVE, jnp.float32)
        stats[side, 1] = jnp.zeros((rows, 128), jnp.float32)
        stats[side, 2] = jnp.zeros((rows, 128), jnp.float32)

    def tile(side, qt, ks, kc, itself=False):
        q_rows = pl.ds(pl.multiple_of(qt * TILE, TILE), TILE)
        k_rows = pl.ds(pl.multiple_of(kc * TILE, TILE), TILE)
        sims = lax.dot_general(
            blocks[2 * side, q_rows, :],
            blocks[ks, k_rows, :],
            (((1,), (1,)), ((), ())),
            preferred_element_type=jnp.float32,
        )
        mask = q_labels[side, q_rows, :] == k_labels[ks, kc]
        if itself:
            row = lax.broadcasted_iota(jnp.int32, (TILE, TILE), 0) + qt * TILE
            col = lax.broadcasted_iota(jnp.int32, (TILE, TILE), 1) + kc * TILE
            mask = mask & (row != col)
        sims = jnp.where(mask, sims, NEGATIVE)
        left, right = sims[:, :128], sims[:, 128:]
        old = stats[side, 0, q_rows, :]
        top = jnp.maximum(old, jnp.maximum(left, right))
        factor = jnp.exp(SCALE * (old - top))
        left_term = jnp.exp(SCALE * (left - top))
        right_term = jnp.exp(SCALE * (right - top))
        stats[side, 0, q_rows, :] = top
        stats[side, 1, q_rows, :] = stats[side, 1, q_rows, :] * factor + (left_term + right_term)
        stats[side, 2, q_rows, :] = stats[side, 2, q_rows, :] * factor + (
            left_term * left + right_term * right
        )

    def each(count, body):
        lax.fori_loop(0, count, lambda i, none: (body(i), none)[1], 0)

    each(tiles * tiles, lambda i: tile(0, i // tiles, 0, i % tiles, itself=True))
    from_sibling.wait()
    each(tiles * tiles, lambda i: tile(0, i // tiles, 1, i % tiles))
    for c in range(tiles):
        for axis in range(2):
            direct[c][axis].wait()
            passed.append(
                send(
                    blocks.at[2 + axis, cut(c), :],
                    blocks.at[4 + axis, cut(c), :],
                    4 * c + 2 + axis,
                    peers[0],
                )
            )
        each(2 * tiles, lambda i: tile(0, i // 2, 2 + i % 2, c))
        each(c + 1, lambda i: tile(1, i, 3, c))
        if c:
            each(c, lambda i: tile(1, c, 3, i))
        passed[2 * c].wait()
        passed[2 * c + 1].wait()
        each(c + 1, lambda i: tile(1, i, 5, c))
        if c:
            each(c, lambda i: tile(1, c, 5, i))
        if c < tiles - 1:
            each(2 * tiles, lambda i: tile(0, i // 2, 4 + i % 2, c))

    def fold(side):
        top = stats[side, 0]
        best = jnp.max(top, axis=1, keepdims=True)
        factor = jnp.exp(SCALE * (top - best))
        total = jnp.sum(stats[side, 1] * factor, axis=1, keepdims=True)
        weight = jnp.sum(stats[side, 2] * factor, axis=1, keepdims=True)
        lane = lax.broadcasted_iota(jnp.int32, (rows, 128), 1)
        packed = jnp.where(lane == 0, best, jnp.where(lane == 1, total, weight))
        return packed.T[:8]

    part[1] = fold(1)
    diagonal = send(part.at[1], theirs, 4 * tiles + 1, peers[1])
    each(2 * tiles, lambda i: tile(0, i // 2, 4 + i % 2, tiles - 1))
    mine = fold(0)
    diagonal.wait()
    other = theirs[...]
    best = jnp.maximum(mine[0:1], other[0:1])
    ours, others = jnp.exp(SCALE * (mine[0:1] - best)), jnp.exp(SCALE * (other[0:1] - best))
    total = mine[1:2] * ours + other[1:2] * others
    weight = mine[2:3] * ours + other[2:3] * others
    line = lax.broadcasted_iota(jnp.int32, (8, rows), 0)
    part[0] = jnp.where(line == 0, best, weight / total)
    home = [
        send(part.at[0], back.at[me], 4 * tiles + 1 + d, peers[2 + d]) for d in range(1, tile_rows)
    ]
    back[me] = part[0]
    for copy in home:
        copy.wait()


def plane_stats(queries, key_labels, place, tile_rows):
    rows, width = queries.shape
    tiles = rows // TILE
    order = [0, 1, 2, 4, 3, 5]
    near = jnp.stack(
        [lax.dynamic_index_in_dim(key_labels, place ^ n, 0, keepdims=False) for n in order]
    )
    vmem = pl.BlockSpec(memory_space=pltpu.VMEM)
    return pl.pallas_call(
        functools.partial(plane_kernel, tile_rows),
        in_specs=[vmem] * 3,
        out_specs=vmem,
        out_shape=jax.ShapeDtypeStruct((tile_rows, 8, rows), jnp.float32),
        scratch_shapes=[
            pltpu.VMEM((6, rows, width), jnp.bfloat16),
            pltpu.VMEM((2, 3, rows, 128), jnp.float32),
            pltpu.VMEM((2, 8, rows), jnp.float32),
            pltpu.VMEM((8, rows), jnp.float32),
            pltpu.SemaphoreType.DMA((2, 4 * tiles + 1 + tile_rows)),
        ],
        compiler_params=pltpu.CompilerParams(
            collective_id=1, has_side_effects=True, vmem_limit_bytes=40 << 20
        ),
    )(near[jnp.array([0, 2])][:, :, None], near.reshape(6, tiles, 1, TILE), queries)


def permute(target, count, parts):
    matrix = (jnp.arange(count, dtype=jnp.int32)[:, None] == target[None, :]).astype(jnp.bfloat16)
    return [
        jnp.dot(matrix, part, preferred_element_type=jnp.float32).astype(jnp.bfloat16)
        for part in parts
    ]


def exclusive(values, axis):
    return jnp.cumsum(values, axis=axis) - values


def per_device(embeddings, labels):
    shard_rows, feature_dim = embeddings.shape
    tile_rows = lax.axis_size("tr")
    columns = lax.axis_size("tc")
    me = lax.axis_index("tr")
    place = lax.axis_index("tc")
    clusters = tile_rows * GROUP_CLUSTERS
    share = shard_rows // tile_rows
    capacity = -(-(share + tile_rows - 1) // 16) * 16
    i32 = jnp.int32

    onehot = labels[:, None] == jnp.arange(clusters, dtype=i32)[None, :]
    held = jnp.sum(onehot.astype(i32), axis=0)
    column, everywhere = gather_counts(held, tile_rows, columns)

    index = jnp.arange(shard_rows, dtype=i32)
    lower = (index[:, None] > index[None, :]).astype(jnp.bfloat16)
    ahead = jnp.dot(lower, onehot.astype(jnp.bfloat16), preferred_element_type=jnp.float32)
    rank = jnp.sum(jnp.where(onehot, ahead, 0.0), axis=1).astype(i32)
    starts = exclusive(held, 0)
    order = jnp.sum(jnp.where(onehot, starts[None, :], 0), axis=1) + rank

    values = embeddings.astype(jnp.float32)
    unit = (values * lax.rsqrt(jnp.sum(values * values, axis=1, keepdims=True) + EPSILON)).astype(
        jnp.bfloat16
    )
    width = feature_dim // CHUNKS
    parts = [unit[:, c * width : (c + 1) * width] for c in range(CHUNKS)]

    def exchange(part, count):
        return lax.all_to_all(
            part.reshape(tile_rows, count, width), "tr", split_axis=0, concat_axis=0, tiled=True
        ).reshape(tile_rows * count, width)

    spread = permute(order % tile_rows * share + order // tile_rows, shard_rows, parts)
    spread = [exchange(part, share) for part in spread]

    local = exclusive(column, 1)
    group_count = column.reshape(tile_rows, tile_rows, GROUP_CLUSTERS).sum(2)
    group_start = exclusive(group_count, 1)
    via = jnp.arange(tile_rows, dtype=i32)

    def before(limit):
        return (limit[..., None] - via + tile_rows - 1) // tile_rows

    first = before(group_start)
    passed = before(group_start + group_count) - first
    base = exclusive(passed, 0) - first

    number = jnp.arange(share, dtype=i32)[None, :] * tile_rows + me
    inside = (number[:, :, None] >= group_start[:, None, :]) & (
        number[:, :, None] < (group_start + group_count)[:, None, :]
    )
    my_base = lax.dynamic_index_in_dim(base, me, 2, keepdims=False)
    lane = my_base[:, None, :] + number[:, :, None] // tile_rows
    target = jnp.sum(jnp.where(inside, via * capacity + lane, 0), axis=2).reshape(-1)
    routed = permute(target, tile_rows * capacity, spread)
    routed = [exchange(part, capacity) for part in routed]

    mine = lax.dynamic_slice_in_dim(column, me * GROUP_CLUSTERS, GROUP_CLUSTERS, 1)
    lengths = mine.T.reshape(-1)
    seg_start = exclusive(lengths, 0)
    seg_local = lax.dynamic_slice_in_dim(local, me * GROUP_CLUSTERS, GROUP_CLUSTERS, 1).T.reshape(-1)
    within = (index[:, None] >= seg_start[None, :]) & (
        index[:, None] < (seg_start + lengths)[None, :]
    )
    number = index + jnp.sum(jnp.where(within, (seg_local - seg_start)[None, :], 0), axis=1)
    route = number % tile_rows
    tables = lax.dynamic_index_in_dim(base, me, 1, keepdims=False)
    tables = jnp.tile(tables, (GROUP_CLUSTERS, 1))
    picked = jnp.sum(jnp.where(within[:, :, None], tables[None], 0), axis=1)
    offset = jnp.sum(jnp.where(route[:, None] == via[None, :], picked, 0), axis=1)
    source = route * capacity + offset + number // tile_rows
    matrix = (
        source[:, None] == jnp.arange(tile_rows * capacity, dtype=i32)[None, :]
    ).astype(jnp.bfloat16)
    queries = [
        jnp.dot(matrix, part, preferred_element_type=jnp.float32).astype(jnp.bfloat16)
        for part in routed
    ]
    totals = lax.dynamic_slice_in_dim(everywhere, me * GROUP_CLUSTERS, GROUP_CLUSTERS, 1)
    ends = jnp.cumsum(totals, axis=1)[:, : GROUP_CLUSTERS - 1]
    key_labels = jnp.sum((index[None, :, None] >= ends[:, None, :]).astype(i32), axis=2)

    if columns == 8:
        back = plane_stats(queries[0], key_labels, place, tile_rows)
        back = jnp.stack([back[:, 0].reshape(-1), back[:, 1].reshape(-1)])
    else:
        keys = [lax.all_gather(part, "tc", axis=0, tiled=True) for part in queries]
        query_labels = lax.dynamic_index_in_dim(key_labels, place, 0, keepdims=False)
        best, weighted = cluster_stats(queries, keys, query_labels, key_labels.reshape(-1), place)
        back = lax.all_gather(jnp.stack([best, weighted]), "tr", axis=1, tiled=True)
    shard_before = exclusive(column, 0)
    begin = exclusive(column.sum(0), 0) + lax.dynamic_index_in_dim(
        shard_before, me, 0, keepdims=False
    )
    position = jnp.sum(jnp.where(onehot, begin[None, :], 0), axis=1) + rank
    here = position[:, None] == jnp.arange(tile_rows * shard_rows, dtype=i32)[None, :]
    best_sim = jnp.sum(jnp.where(here, back[0][None, :], 0.0), axis=1)
    mean_sim = jnp.sum(jnp.where(here, back[1][None, :], 0.0), axis=1)
    flag = jax.nn.sigmoid(SHARPNESS * (best_sim - THRESHOLD))
    return (best_sim, mean_sim, flag)


def solution(mesh):
    placed = (P(("tr", "tc"), None), P(("tr", "tc")))
    return jax.shard_map(
        per_device,
        mesh=mesh,
        in_specs=placed,
        out_specs=(P(("tr", "tc")), P(("tr", "tc")), P(("tr", "tc"))),
        check_vma=False,
    )
```

```python
import functools

import jax
import jax.numpy as jnp
from jax import lax
from jax.experimental import pallas as pl
from jax.experimental.pallas import tpu as pltpu
from jax.sharding import PartitionSpec as P

GROUP_CLUSTERS = 4


SCALE = 256.0
NEGATIVE = -1e30
EPSILON = 1e-06
THRESHOLD = 0.3
SHARPNESS = 50.0
TILE = 256
MESH = pl.DeviceIdType.MESH


def stats_kernel(chunks, q_lo, q_hi, k_lo, k_hi, place, q_labels, k_labels, *refs):
    queries, keys = refs[:chunks], refs[chunks : 2 * chunks]
    best_ref, weighted_ref, sims_ref, top_ref = refs[2 * chunks :]
    block = pl.program_id(0)
    rows = queries[0].shape[0]
    tiles = rows // TILE

    @pl.when(block == 0)
    def _():
        top_ref[...] = jnp.full(top_ref.shape, NEGATIVE, jnp.float32)

    for kt in range(tiles):
        kn = block * tiles + kt
        for qt in range(tiles):
            own = block == place[0]
            q_rows = pl.ds(qt * TILE, TILE)
            k_rows = pl.ds(kt * TILE, TILE)

            @pl.when((q_lo[qt] <= k_hi[kn]) & (k_lo[kn] <= q_hi[qt]))
            def _():
                sims = None
                for c in range(chunks):
                    part = lax.dot_general(
                        queries[c][q_rows, :],
                        keys[c][k_rows, :],
                        (((1,), (1,)), ((), ())),
                        preferred_element_type=jnp.float32,
                    )
                    sims = part if sims is None else sims + part
                mask = q_labels[q_rows, :] == k_labels[0, :, k_rows]
                if qt == kt:
                    row = lax.broadcasted_iota(jnp.int32, (TILE, TILE), 0)
                    col = lax.broadcasted_iota(jnp.int32, (TILE, TILE), 1)
                    mask = mask & ((row != col) | jnp.logical_not(own))
                sims = jnp.where(mask, sims, NEGATIVE)
                sims_ref[kn, q_rows, :] = sims
                part = jnp.maximum(sims[:, :128], sims[:, 128:])
                top_ref[q_rows, :] = jnp.maximum(top_ref[q_rows, :], part)

    @pl.when(block == pl.num_programs(0) - 1)
    def _():
        for qt in range(tiles):
            q_rows = pl.ds(qt * TILE, TILE)
            best = jnp.max(top_ref[q_rows, :], axis=1, keepdims=True)

            def step(kn, carry):
                def visit(carry):
                    total, weight = carry
                    sims = sims_ref[kn, q_rows, :]
                    terms = jnp.exp(SCALE * (sims - best))
                    both = terms * sims
                    return (
                        total + (terms[:, :128] + terms[:, 128:]),
                        weight + (both[:, :128] + both[:, 128:]),
                    )

                meets = (q_lo[qt] <= k_hi[kn]) & (k_lo[kn] <= q_hi[qt])
                return lax.cond(meets, visit, lambda same: same, carry)

            zero = jnp.zeros((TILE, 128), jnp.float32)
            total, weight = lax.fori_loop(0, sims_ref.shape[0], step, (zero, zero))
            best_ref[q_rows, :] = best
            weighted_ref[q_rows, :] = jnp.sum(weight, axis=1, keepdims=True) / jnp.sum(
                total, axis=1, keepdims=True
            )


def cluster_stats(queries, keys, query_labels, key_labels, place):
    chunks = len(queries)
    rows, width = queries[0].shape
    members = keys[0].shape[0]
    q_tiles = query_labels.reshape(-1, TILE)
    k_tiles = key_labels.reshape(-1, TILE)
    smem = pl.BlockSpec(memory_space=pltpu.SMEM)
    scratch = rows * members * 4
    best, weighted = pl.pallas_call(
        functools.partial(stats_kernel, chunks),
        grid=(members // rows,),
        in_specs=[smem] * 5
        + [
            pl.BlockSpec((rows, 1), lambda b: (0, 0)),
            pl.BlockSpec((1, 1, rows), lambda b: (b, 0, 0)),
        ]
        + [pl.BlockSpec((rows, width), lambda b: (0, 0))] * chunks
        + [pl.BlockSpec((rows, width), lambda b: (b, 0))] * chunks,
        out_specs=[pl.BlockSpec((rows, 1), lambda b: (0, 0))] * 2,
        out_shape=[jax.ShapeDtypeStruct((rows, 1), jnp.float32)] * 2,
        scratch_shapes=[
            pltpu.VMEM((members // TILE, rows, TILE), jnp.float32),
            pltpu.VMEM((rows, 128), jnp.float32),
        ],
        compiler_params=pltpu.CompilerParams(vmem_limit_bytes=scratch + (16 << 20)),
        cost_estimate=pl.CostEstimate(
            flops=2 * rows * members * width * chunks,
            bytes_accessed=2 * members * width * chunks,
            transcendentals=rows * members,
        ),
    )(
        q_tiles[:, 0],
        q_tiles[:, -1],
        k_tiles[:, 0],
        k_tiles[:, -1],
        place.reshape(1),
        query_labels[:, None],
        key_labels.reshape(-1, 1, rows),
        *queries,
        *keys,
    )
    return best[:, 0], weighted[:, 0]


def count_kernel(rows, columns, held, column, totals, mine, sems):
    me, place = lax.axis_index("tr"), lax.axis_index("tc")
    tr_peers = [lax.rem(me + d, rows) for d in range(1, rows)]
    tc_peers = [lax.rem(place + d, columns) for d in range(1, columns)]
    barrier = pltpu.get_barrier_semaphore()
    for peer in tr_peers:
        pl.semaphore_signal(barrier, inc=1, device_id=(peer, place), device_id_type=MESH)
    for peer in tc_peers:
        pl.semaphore_signal(barrier, inc=1, device_id=(me, peer), device_id_type=MESH)
    pl.semaphore_wait(barrier, rows + columns - 2)

    def exchange(source, buffer, index, peers, first, whom):
        copies = []
        for d, peer in enumerate(peers):
            copy = pltpu.make_async_remote_copy(
                src_ref=source,
                dst_ref=buffer.at[index],
                send_sem=sems.at[0, first + d],
                recv_sem=sems.at[1, first + d],
                device_id=whom(peer),
                device_id_type=MESH,
            )
            copy.start()
            copies.append(copy)
        buffer[index] = source[...]
        for copy in copies:
            copy.wait()

    exchange(held, column, me, tr_peers, 0, lambda peer: (peer, place))
    mine[...] = jnp.sum(column[...], axis=0)
    exchange(mine, totals, place, tc_peers, rows - 1, lambda peer: (me, peer))


def gather_counts(held, rows, columns):
    clusters = held.shape[0]
    padded = jnp.zeros((8, 128), jnp.int32).at[0, :clusters].set(held)
    vmem = pl.BlockSpec(memory_space=pltpu.VMEM)
    column, totals = pl.pallas_call(
        functools.partial(count_kernel, rows, columns),
        in_specs=[vmem],
        out_specs=[vmem, vmem],
        out_shape=[
            jax.ShapeDtypeStruct((rows, 8, 128), jnp.int32),
            jax.ShapeDtypeStruct((columns, 8, 128), jnp.int32),
        ],
        scratch_shapes=[
            pltpu.VMEM((8, 128), jnp.int32),
            pltpu.SemaphoreType.DMA((2, rows + columns - 2)),
        ],
        compiler_params=pltpu.CompilerParams(collective_id=0, has_side_effects=True),
    )(padded)
    return column[:, 0, :clusters], totals[:, 0, :clusters]


def plane_kernel(
    tile_rows,
    q_labels,
    k_labels,
    unit,
    spread,
    route,
    settle,
    back,
    sent,
    landed,
    routed,
    arrived,
    blocks,
    stats,
    part,
    theirs,
    sems,
):
    me, place = lax.axis_index("tr"), lax.axis_index("tc")
    sibling = place + 1 - 2 * (place % 2)
    across = place + 2 - 4 * ((place // 2) % 2)
    along = place + 4 - 8 * (place // 4)
    rows, width = unit.shape
    tiles = rows // TILE
    share = rows // tile_rows
    capacity = routed.shape[0] // tile_rows
    pieces = width // TILE
    peers = [(me, sibling), (me, across), (me, along)]
    others = [lax.rem(me + d, tile_rows) for d in range(1, tile_rows)]
    peers += [(other, place) for other in others]
    barrier = pltpu.get_barrier_semaphore()
    for peer in peers:
        pl.semaphore_signal(barrier, inc=1, device_id=peer, device_id_type=MESH)
    pl.semaphore_wait(barrier, len(peers))
    counter = iter(range(sems.shape[1]))

    def send(source, target, peer):
        number = next(counter)
        copy = pltpu.make_async_remote_copy(
            src_ref=source,
            dst_ref=target,
            send_sem=sems.at[0, number],
            recv_sem=sems.at[1, number],
            device_id=peer,
            device_id_type=MESH,
        )
        copy.start()
        return copy

    def exchange(source, target, count, lanes):
        def slot(row):
            return pl.ds(pl.multiple_of(row * count, 16), count)

        copies = [
            send(source.at[slot(other), lanes], target.at[slot(me), lanes], (other, place))
            for other in others
        ]
        target[slot(me), lanes] = source[slot(me), lanes]
        return copies

    def move(matrix, source, lanes):
        return jnp.dot(
            matrix[...], source[:, lanes], preferred_element_type=jnp.float32
        ).astype(jnp.bfloat16)

    lanes = [pl.ds(f * TILE, TILE) for f in range(pieces)]
    first, second, direct, from_sibling, passed = [], [], [], [], []
    for f in range(pieces):
        sent[:, lanes[f]] = move(spread, unit, lanes[f])
        first.append(exchange(sent, landed, share, lanes[f]))
    for side in range(2):
        stats[side, 0] = jnp.full((rows, 128), NEGATIVE, jnp.float32)
        stats[side, 1] = jnp.zeros((rows, 128), jnp.float32)
        stats[side, 2] = jnp.zeros((rows, 128), jnp.float32)
    for f in range(pieces):
        for copy in first[f]:
            copy.wait()
        routed[:, lanes[f]] = move(route, landed, lanes[f])
        second.append(exchange(routed, arrived, capacity, lanes[f]))

    def forward(f):
        for axis in range(2):
            direct[f][axis].wait()
            passed.append(
                send(
                    blocks.at[2 + axis, :, lanes[f]], blocks.at[4 + axis, :, lanes[f]], peers[0]
                )
            )

    for f in range(pieces):
        for copy in second[f]:
            copy.wait()
        blocks[0, :, lanes[f]] = move(settle, arrived, lanes[f])
        own = blocks.at[0, :, lanes[f]]
        direct.append(
            [
                send(own, blocks.at[2, :, lanes[f]], peers[1]),
                send(own, blocks.at[3, :, lanes[f]], peers[2]),
            ]
        )
        from_sibling.append(send(own, blocks.at[1, :, lanes[f]], peers[0]))
        if f:
            forward(f - 1)

    def tile(side, qt, ks, kc, itself=False):
        q_rows = pl.ds(pl.multiple_of(qt * TILE, TILE), TILE)
        k_rows = pl.ds(pl.multiple_of(kc * TILE, TILE), TILE)
        sims = lax.dot_general(
            blocks[2 * side, q_rows, :],
            blocks[ks, k_rows, :],
            (((1,), (1,)), ((), ())),
            preferred_element_type=jnp.float32,
        )
        mask = q_labels[side, q_rows, :] == k_labels[ks, kc]
        if itself:
            row = lax.broadcasted_iota(jnp.int32, (TILE, TILE), 0) + qt * TILE
            col = lax.broadcasted_iota(jnp.int32, (TILE, TILE), 1) + kc * TILE
            mask = mask & (row != col)
        sims = jnp.where(mask, sims, NEGATIVE)
        left, right = sims[:, :128], sims[:, 128:]
        old = stats[side, 0, q_rows, :]
        top = jnp.maximum(old, jnp.maximum(left, right))
        factor = jnp.exp(SCALE * (old - top))
        left_term = jnp.exp(SCALE * (left - top))
        right_term = jnp.exp(SCALE * (right - top))
        stats[side, 0, q_rows, :] = top
        stats[side, 1, q_rows, :] = stats[side, 1, q_rows, :] * factor + (left_term + right_term)
        stats[side, 2, q_rows, :] = stats[side, 2, q_rows, :] * factor + (
            left_term * left + right_term * right
        )

    def each(count, body):
        lax.fori_loop(0, count, lambda i, none: (body(i), none)[1], 0)

    square = tiles * tiles
    each(square, lambda i: tile(0, i // tiles, 0, i % tiles, itself=True))
    forward(pieces - 1)
    for copy in from_sibling:
        copy.wait()
    each(square, lambda i: tile(0, i // tiles, 1, i % tiles))
    each(2 * square, lambda i: tile(0, i // 2 % tiles, 2 + i % 2, i // 2 // tiles))
    each(square, lambda i: tile(1, i // tiles, 3, i % tiles))
    for copy in passed:
        copy.wait()
    each(square, lambda i: tile(1, i // tiles, 5, i % tiles))

    def fold(side):
        top = stats[side, 0]
        best = jnp.max(top, axis=1, keepdims=True)
        factor = jnp.exp(SCALE * (top - best))
        total = jnp.sum(stats[side, 1] * factor, axis=1, keepdims=True)
        weight = jnp.sum(stats[side, 2] * factor, axis=1, keepdims=True)
        lane = lax.broadcasted_iota(jnp.int32, (rows, 128), 1)
        packed = jnp.where(lane == 0, best, jnp.where(lane == 1, total, weight))
        return packed.T[:8]

    part[1] = fold(1)
    diagonal = send(part.at[1], theirs, peers[1])
    each(2 * square, lambda i: tile(0, i // 2 % tiles, 4 + i % 2, i // 2 // tiles))
    mine = fold(0)
    diagonal.wait()
    other = theirs[...]
    best = jnp.maximum(mine[0:1], other[0:1])
    ours, others = jnp.exp(SCALE * (mine[0:1] - best)), jnp.exp(SCALE * (other[0:1] - best))
    total = mine[1:2] * ours + other[1:2] * others
    weight = mine[2:3] * ours + other[2:3] * others
    line = lax.broadcasted_iota(jnp.int32, (8, rows), 0)
    part[0] = jnp.where(line == 0, best, weight / total)
    home = [send(part.at[0], back.at[me], peer) for peer in peers[3:]]
    back[me] = part[0]
    for copy in home:
        copy.wait()


def plane_stats(unit, spread, route, settle, key_labels, place, tile_rows):
    rows, width = unit.shape
    tiles = rows // TILE
    padded = route.shape[0]
    copies = width // TILE * (2 * (tile_rows - 1) + 5) + tile_rows
    order = [0, 1, 2, 4, 3, 5]
    near = jnp.stack(
        [lax.dynamic_index_in_dim(key_labels, place ^ n, 0, keepdims=False) for n in order]
    )
    vmem = pl.BlockSpec(memory_space=pltpu.VMEM)
    return pl.pallas_call(
        functools.partial(plane_kernel, tile_rows),
        in_specs=[vmem] * 6,
        out_specs=vmem,
        out_shape=jax.ShapeDtypeStruct((tile_rows, 8, rows), jnp.float32),
        scratch_shapes=[
            pltpu.VMEM((rows, width), jnp.bfloat16),
            pltpu.VMEM((rows, width), jnp.bfloat16),
            pltpu.VMEM((padded, width), jnp.bfloat16),
            pltpu.VMEM((padded, width), jnp.bfloat16),
            pltpu.VMEM((6, rows, width), jnp.bfloat16),
            pltpu.VMEM((2, 3, rows, 128), jnp.float32),
            pltpu.VMEM((2, 8, rows), jnp.float32),
            pltpu.VMEM((8, rows), jnp.float32),
            pltpu.SemaphoreType.DMA((2, copies)),
        ],
        compiler_params=pltpu.CompilerParams(
            collective_id=1, has_side_effects=True, vmem_limit_bytes=48 << 20
        ),
    )(
        near[jnp.array([0, 2])][:, :, None],
        near.reshape(6, tiles, 1, TILE),
        unit,
        spread,
        route,
        settle,
    )


def placing(target, count):
    return (jnp.arange(count, dtype=jnp.int32)[:, None] == target[None, :]).astype(jnp.bfloat16)


def permute(matrix, part):
    return jnp.dot(matrix, part, preferred_element_type=jnp.float32).astype(jnp.bfloat16)


def exclusive(values, axis):
    return jnp.cumsum(values, axis=axis) - values


def per_device(embeddings, labels):
    shard_rows, feature_dim = embeddings.shape
    tile_rows = lax.axis_size("tr")
    columns = lax.axis_size("tc")
    me = lax.axis_index("tr")
    place = lax.axis_index("tc")
    clusters = tile_rows * GROUP_CLUSTERS
    share = shard_rows // tile_rows
    capacity = -(-(share + tile_rows - 1) // 16) * 16
    i32 = jnp.int32

    onehot = labels[:, None] == jnp.arange(clusters, dtype=i32)[None, :]
    held = jnp.sum(onehot.astype(i32), axis=0)
    column, everywhere = gather_counts(held, tile_rows, columns)

    index = jnp.arange(shard_rows, dtype=i32)
    lower = (index[:, None] > index[None, :]).astype(jnp.bfloat16)
    ahead = jnp.dot(lower, onehot.astype(jnp.bfloat16), preferred_element_type=jnp.float32)
    rank = jnp.sum(jnp.where(onehot, ahead, 0.0), axis=1).astype(i32)
    starts = exclusive(held, 0)
    order = jnp.sum(jnp.where(onehot, starts[None, :], 0), axis=1) + rank

    values = embeddings.astype(jnp.float32)
    unit = (values * lax.rsqrt(jnp.sum(values * values, axis=1, keepdims=True) + EPSILON)).astype(
        jnp.bfloat16
    )

    def exchange(part, count):
        return lax.all_to_all(
            part.reshape(tile_rows, count, feature_dim),
            "tr",
            split_axis=0,
            concat_axis=0,
            tiled=True,
        ).reshape(tile_rows * count, feature_dim)

    spread = placing(order % tile_rows * share + order // tile_rows, shard_rows)

    local = exclusive(column, 1)
    group_count = column.reshape(tile_rows, tile_rows, GROUP_CLUSTERS).sum(2)
    group_start = exclusive(group_count, 1)
    via = jnp.arange(tile_rows, dtype=i32)

    def before(limit):
        return (limit[..., None] - via + tile_rows - 1) // tile_rows

    first = before(group_start)
    passed = before(group_start + group_count) - first
    base = exclusive(passed, 0) - first

    number = jnp.arange(share, dtype=i32)[None, :] * tile_rows + me
    inside = (number[:, :, None] >= group_start[:, None, :]) & (
        number[:, :, None] < (group_start + group_count)[:, None, :]
    )
    my_base = lax.dynamic_index_in_dim(base, me, 2, keepdims=False)
    lane = my_base[:, None, :] + number[:, :, None] // tile_rows
    target = jnp.sum(jnp.where(inside, via * capacity + lane, 0), axis=2).reshape(-1)
    route = placing(target, tile_rows * capacity)

    mine = lax.dynamic_slice_in_dim(column, me * GROUP_CLUSTERS, GROUP_CLUSTERS, 1)
    lengths = mine.T.reshape(-1)
    seg_start = exclusive(lengths, 0)
    seg_local = lax.dynamic_slice_in_dim(local, me * GROUP_CLUSTERS, GROUP_CLUSTERS, 1).T.reshape(-1)
    within = (index[:, None] >= seg_start[None, :]) & (
        index[:, None] < (seg_start + lengths)[None, :]
    )
    number = index + jnp.sum(jnp.where(within, (seg_local - seg_start)[None, :], 0), axis=1)
    way = number % tile_rows
    tables = lax.dynamic_index_in_dim(base, me, 1, keepdims=False)
    tables = jnp.tile(tables, (GROUP_CLUSTERS, 1))
    picked = jnp.sum(jnp.where(within[:, :, None], tables[None], 0), axis=1)
    offset = jnp.sum(jnp.where(way[:, None] == via[None, :], picked, 0), axis=1)
    source = way * capacity + offset + number // tile_rows
    settle = (
        source[:, None] == jnp.arange(tile_rows * capacity, dtype=i32)[None, :]
    ).astype(jnp.bfloat16)

    totals = lax.dynamic_slice_in_dim(everywhere, me * GROUP_CLUSTERS, GROUP_CLUSTERS, 1)
    ends = jnp.cumsum(totals, axis=1)[:, : GROUP_CLUSTERS - 1]
    key_labels = jnp.sum((index[None, :, None] >= ends[:, None, :]).astype(i32), axis=2)

    if columns == 8:
        back = plane_stats(unit, spread, route, settle, key_labels, place, tile_rows)
        back = jnp.stack([back[:, 0].reshape(-1), back[:, 1].reshape(-1)])
    else:
        landed = exchange(permute(spread, unit), share)
        arrived = exchange(permute(route, landed), capacity)
        queries = permute(settle, arrived)
        keys = lax.all_gather(queries, "tc", axis=0, tiled=True)
        query_labels = lax.dynamic_index_in_dim(key_labels, place, 0, keepdims=False)
        best, weighted = cluster_stats([queries], [keys], query_labels, key_labels.reshape(-1), place)
        back = lax.all_gather(jnp.stack([best, weighted]), "tr", axis=1, tiled=True)
    shard_before = exclusive(column, 0)
    begin = exclusive(column.sum(0), 0) + lax.dynamic_index_in_dim(
        shard_before, me, 0, keepdims=False
    )
    position = jnp.sum(jnp.where(onehot, begin[None, :], 0), axis=1) + rank
    here = position[:, None] == jnp.arange(tile_rows * shard_rows, dtype=i32)[None, :]
    best_sim = jnp.sum(jnp.where(here, back[0][None, :], 0.0), axis=1)
    mean_sim = jnp.sum(jnp.where(here, back[1][None, :], 0.0), axis=1)
    flag = jax.nn.sigmoid(SHARPNESS * (best_sim - THRESHOLD))
    return (best_sim, mean_sim, flag)


def solution(mesh):
    placed = (P(("tr", "tc"), None), P(("tr", "tc")))
    return jax.shard_map(
        per_device,
        mesh=mesh,
        in_specs=placed,
        out_specs=(P(("tr", "tc")), P(("tr", "tc")), P(("tr", "tc"))),
        check_vma=False,
    )
```

```python
import functools

import jax
import jax.numpy as jnp
from jax import lax
from jax.experimental import pallas as pl
from jax.experimental.pallas import tpu as pltpu
from jax.sharding import PartitionSpec as P

GROUP_CLUSTERS = 4


SCALE = 256.0
NEGATIVE = -1e30
EPSILON = 1e-06
THRESHOLD = 0.3
SHARPNESS = 50.0
TILE = 256
MESH = pl.DeviceIdType.MESH


def stats_kernel(chunks, q_lo, q_hi, k_lo, k_hi, place, q_labels, k_labels, *refs):
    queries, keys = refs[:chunks], refs[chunks : 2 * chunks]
    best_ref, weighted_ref, sims_ref, top_ref = refs[2 * chunks :]
    block = pl.program_id(0)
    rows = queries[0].shape[0]
    tiles = rows // TILE

    @pl.when(block == 0)
    def _():
        top_ref[...] = jnp.full(top_ref.shape, NEGATIVE, jnp.float32)

    for kt in range(tiles):
        kn = block * tiles + kt
        for qt in range(tiles):
            own = block == place[0]
            q_rows = pl.ds(qt * TILE, TILE)
            k_rows = pl.ds(kt * TILE, TILE)

            @pl.when((q_lo[qt] <= k_hi[kn]) & (k_lo[kn] <= q_hi[qt]))
            def _():
                sims = None
                for c in range(chunks):
                    part = lax.dot_general(
                        queries[c][q_rows, :],
                        keys[c][k_rows, :],
                        (((1,), (1,)), ((), ())),
                        preferred_element_type=jnp.float32,
                    )
                    sims = part if sims is None else sims + part
                mask = q_labels[q_rows, :] == k_labels[0, :, k_rows]
                if qt == kt:
                    row = lax.broadcasted_iota(jnp.int32, (TILE, TILE), 0)
                    col = lax.broadcasted_iota(jnp.int32, (TILE, TILE), 1)
                    mask = mask & ((row != col) | jnp.logical_not(own))
                sims = jnp.where(mask, sims, NEGATIVE)
                sims_ref[kn, q_rows, :] = sims
                part = jnp.maximum(sims[:, :128], sims[:, 128:])
                top_ref[q_rows, :] = jnp.maximum(top_ref[q_rows, :], part)

    @pl.when(block == pl.num_programs(0) - 1)
    def _():
        for qt in range(tiles):
            q_rows = pl.ds(qt * TILE, TILE)
            best = jnp.max(top_ref[q_rows, :], axis=1, keepdims=True)

            def step(kn, carry):
                def visit(carry):
                    total, weight = carry
                    sims = sims_ref[kn, q_rows, :]
                    terms = jnp.exp(SCALE * (sims - best))
                    both = terms * sims
                    return (
                        total + (terms[:, :128] + terms[:, 128:]),
                        weight + (both[:, :128] + both[:, 128:]),
                    )

                meets = (q_lo[qt] <= k_hi[kn]) & (k_lo[kn] <= q_hi[qt])
                return lax.cond(meets, visit, lambda same: same, carry)

            zero = jnp.zeros((TILE, 128), jnp.float32)
            total, weight = lax.fori_loop(0, sims_ref.shape[0], step, (zero, zero))
            best_ref[q_rows, :] = best
            weighted_ref[q_rows, :] = jnp.sum(weight, axis=1, keepdims=True) / jnp.sum(
                total, axis=1, keepdims=True
            )


def cluster_stats(queries, keys, query_labels, key_labels, place):
    chunks = len(queries)
    rows, width = queries[0].shape
    members = keys[0].shape[0]
    q_tiles = query_labels.reshape(-1, TILE)
    k_tiles = key_labels.reshape(-1, TILE)
    smem = pl.BlockSpec(memory_space=pltpu.SMEM)
    scratch = rows * members * 4
    best, weighted = pl.pallas_call(
        functools.partial(stats_kernel, chunks),
        grid=(members // rows,),
        in_specs=[smem] * 5
        + [
            pl.BlockSpec((rows, 1), lambda b: (0, 0)),
            pl.BlockSpec((1, 1, rows), lambda b: (b, 0, 0)),
        ]
        + [pl.BlockSpec((rows, width), lambda b: (0, 0))] * chunks
        + [pl.BlockSpec((rows, width), lambda b: (b, 0))] * chunks,
        out_specs=[pl.BlockSpec((rows, 1), lambda b: (0, 0))] * 2,
        out_shape=[jax.ShapeDtypeStruct((rows, 1), jnp.float32)] * 2,
        scratch_shapes=[
            pltpu.VMEM((members // TILE, rows, TILE), jnp.float32),
            pltpu.VMEM((rows, 128), jnp.float32),
        ],
        compiler_params=pltpu.CompilerParams(vmem_limit_bytes=scratch + (16 << 20)),
        cost_estimate=pl.CostEstimate(
            flops=2 * rows * members * width * chunks,
            bytes_accessed=2 * members * width * chunks,
            transcendentals=rows * members,
        ),
    )(
        q_tiles[:, 0],
        q_tiles[:, -1],
        k_tiles[:, 0],
        k_tiles[:, -1],
        place.reshape(1),
        query_labels[:, None],
        key_labels.reshape(-1, 1, rows),
        *queries,
        *keys,
    )
    return best[:, 0], weighted[:, 0]


def count_kernel(rows, columns, held, column, totals, mine, sems):
    me, place = lax.axis_index("tr"), lax.axis_index("tc")
    tr_peers = [lax.rem(me + d, rows) for d in range(1, rows)]
    tc_peers = [lax.rem(place + d, columns) for d in range(1, columns)]
    barrier = pltpu.get_barrier_semaphore()
    for peer in tr_peers:
        pl.semaphore_signal(barrier, inc=1, device_id=(peer, place), device_id_type=MESH)
    for peer in tc_peers:
        pl.semaphore_signal(barrier, inc=1, device_id=(me, peer), device_id_type=MESH)
    pl.semaphore_wait(barrier, rows + columns - 2)

    def exchange(source, buffer, index, peers, first, whom):
        copies = []
        for d, peer in enumerate(peers):
            copy = pltpu.make_async_remote_copy(
                src_ref=source,
                dst_ref=buffer.at[index],
                send_sem=sems.at[0, first + d],
                recv_sem=sems.at[1, first + d],
                device_id=whom(peer),
                device_id_type=MESH,
            )
            copy.start()
            copies.append(copy)
        buffer[index] = source[...]
        for copy in copies:
            copy.wait()

    exchange(held, column, me, tr_peers, 0, lambda peer: (peer, place))
    mine[...] = jnp.sum(column[...], axis=0)
    exchange(mine, totals, place, tc_peers, rows - 1, lambda peer: (me, peer))


def gather_counts(held, rows, columns):
    clusters = held.shape[0]
    padded = jnp.zeros((8, 128), jnp.int32).at[0, :clusters].set(held)
    vmem = pl.BlockSpec(memory_space=pltpu.VMEM)
    column, totals = pl.pallas_call(
        functools.partial(count_kernel, rows, columns),
        in_specs=[vmem],
        out_specs=[vmem, vmem],
        out_shape=[
            jax.ShapeDtypeStruct((rows, 8, 128), jnp.int32),
            jax.ShapeDtypeStruct((columns, 8, 128), jnp.int32),
        ],
        scratch_shapes=[
            pltpu.VMEM((8, 128), jnp.int32),
            pltpu.SemaphoreType.DMA((2, rows + columns - 2)),
        ],
        compiler_params=pltpu.CompilerParams(collective_id=0, has_side_effects=True),
    )(padded)
    return column[:, 0, :clusters], totals[:, 0, :clusters]


def plane_kernel(
    tile_rows,
    q_labels,
    k_labels,
    unit,
    spread,
    route,
    settle,
    back,
    sent,
    landed,
    routed,
    arrived,
    blocks,
    stats,
    part,
    theirs,
    sems,
):
    me, place = lax.axis_index("tr"), lax.axis_index("tc")
    sibling = place + 1 - 2 * (place % 2)
    across = place + 2 - 4 * ((place // 2) % 2)
    along = place + 4 - 8 * (place // 4)
    rows, width = unit.shape
    tiles = rows // TILE
    share = rows // tile_rows
    capacity = routed.shape[0] // tile_rows
    pieces = width // TILE
    peers = [(me, sibling), (me, across), (me, along)]
    others = [lax.rem(me + d, tile_rows) for d in range(1, tile_rows)]
    peers += [(other, place) for other in others]
    barrier = pltpu.get_barrier_semaphore()
    for peer in peers:
        pl.semaphore_signal(barrier, inc=1, device_id=peer, device_id_type=MESH)
    pl.semaphore_wait(barrier, len(peers))
    counter = iter(range(sems.shape[1]))

    def send(source, target, peer):
        number = next(counter)
        copy = pltpu.make_async_remote_copy(
            src_ref=source,
            dst_ref=target,
            send_sem=sems.at[0, number],
            recv_sem=sems.at[1, number],
            device_id=peer,
            device_id_type=MESH,
        )
        copy.start()
        return copy

    def exchange(source, target, count, lanes):
        def slot(row):
            return pl.ds(pl.multiple_of(row * count, 16), count)

        copies = [
            send(source.at[slot(other), lanes], target.at[slot(me), lanes], (other, place))
            for other in others
        ]
        target[slot(me), lanes] = source[slot(me), lanes]
        return copies

    def move(matrix, source, lanes):
        return jnp.dot(
            matrix[...], source[:, lanes], preferred_element_type=jnp.float32
        ).astype(jnp.bfloat16)

    lanes = [pl.ds(f * TILE, TILE) for f in range(pieces)]
    first, second, direct, from_sibling, passed = [], [], [], [], []
    for f in range(pieces):
        sent[:, lanes[f]] = move(spread, unit, lanes[f])
        first.append(exchange(sent, landed, share, lanes[f]))
    for side in range(2):
        stats[side, 0] = jnp.full((rows, 128), NEGATIVE, jnp.float32)
        stats[side, 1] = jnp.zeros((rows, 128), jnp.float32)
        stats[side, 2] = jnp.zeros((rows, 128), jnp.float32)
    for f in range(pieces):
        for copy in first[f]:
            copy.wait()
        routed[:, lanes[f]] = move(route, landed, lanes[f])
        second.append(exchange(routed, arrived, capacity, lanes[f]))

    def forward(f):
        for axis in range(2):
            direct[f][axis].wait()
            passed.append(
                send(
                    blocks.at[2 + axis, :, lanes[f]], blocks.at[4 + axis, :, lanes[f]], peers[0]
                )
            )

    for f in range(pieces):
        for copy in second[f]:
            copy.wait()
        blocks[0, :, lanes[f]] = move(settle, arrived, lanes[f])
        own = blocks.at[0, :, lanes[f]]
        direct.append(
            [
                send(own, blocks.at[2, :, lanes[f]], peers[1]),
                send(own, blocks.at[3, :, lanes[f]], peers[2]),
            ]
        )
        from_sibling.append(send(own, blocks.at[1, :, lanes[f]], peers[0]))
        if f:
            forward(f - 1)

    def strip(side, qt, ks, itself=False):
        q_rows = pl.ds(pl.multiple_of(qt * TILE, TILE), TILE)
        sims = lax.dot_general(
            blocks[2 * side, q_rows, :],
            blocks[ks],
            (((1,), (1,)), ((), ())),
            preferred_element_type=jnp.float32,
        )
        mask = q_labels[side, q_rows, :] == k_labels[ks]
        if itself:
            row = lax.broadcasted_iota(jnp.int32, (TILE, rows), 0) + qt * TILE
            col = lax.broadcasted_iota(jnp.int32, (TILE, rows), 1)
            mask = mask & (row != col)
        sims = jnp.where(mask, sims, NEGATIVE)
        pieces = [sims[:, n * 128 : (n + 1) * 128] for n in range(rows // 128)]
        old = stats[side, 0, q_rows, :]
        top = functools.reduce(jnp.maximum, pieces, old)
        factor = jnp.exp(SCALE * (old - top))
        total = stats[side, 1, q_rows, :] * factor
        weight = stats[side, 2, q_rows, :] * factor
        for piece in pieces:
            term = jnp.exp(SCALE * (piece - top))
            total = total + term
            weight = weight + term * piece
        stats[side, 0, q_rows, :] = top
        stats[side, 1, q_rows, :] = total
        stats[side, 2, q_rows, :] = weight

    def each(body):
        lax.fori_loop(0, tiles, lambda i, none: (body(i), none)[1], 0, unroll=True)

    each(lambda i: strip(0, i, 0, itself=True))
    forward(pieces - 1)
    for copy in from_sibling:
        copy.wait()
    each(lambda i: strip(0, i, 1))
    each(lambda i: strip(0, i, 2))
    each(lambda i: strip(0, i, 3))
    each(lambda i: strip(1, i, 3))
    for copy in passed:
        copy.wait()
    each(lambda i: strip(1, i, 5))

    def fold(side):
        top = stats[side, 0]
        best = jnp.max(top, axis=1, keepdims=True)
        factor = jnp.exp(SCALE * (top - best))
        total = jnp.sum(stats[side, 1] * factor, axis=1, keepdims=True)
        weight = jnp.sum(stats[side, 2] * factor, axis=1, keepdims=True)
        lane = lax.broadcasted_iota(jnp.int32, (rows, 128), 1)
        packed = jnp.where(lane == 0, best, jnp.where(lane == 1, total, weight))
        return packed.T[:8]

    part[1] = fold(1)
    diagonal = send(part.at[1], theirs, peers[1])
    each(lambda i: strip(0, i, 4))
    each(lambda i: strip(0, i, 5))
    mine = fold(0)
    diagonal.wait()
    other = theirs[...]
    best = jnp.maximum(mine[0:1], other[0:1])
    ours, others = jnp.exp(SCALE * (mine[0:1] - best)), jnp.exp(SCALE * (other[0:1] - best))
    total = mine[1:2] * ours + other[1:2] * others
    weight = mine[2:3] * ours + other[2:3] * others
    line = lax.broadcasted_iota(jnp.int32, (8, rows), 0)
    part[0] = jnp.where(line == 0, best, weight / total)
    home = [send(part.at[0], back.at[me], peer) for peer in peers[3:]]
    back[me] = part[0]
    for copy in home:
        copy.wait()


def plane_stats(unit, spread, route, settle, key_labels, place, tile_rows):
    rows, width = unit.shape
    tiles = rows // TILE
    padded = route.shape[0]
    copies = width // TILE * (2 * (tile_rows - 1) + 5) + tile_rows
    order = [0, 1, 2, 4, 3, 5]
    near = jnp.stack(
        [lax.dynamic_index_in_dim(key_labels, place ^ n, 0, keepdims=False) for n in order]
    )
    vmem = pl.BlockSpec(memory_space=pltpu.VMEM)
    return pl.pallas_call(
        functools.partial(plane_kernel, tile_rows),
        in_specs=[vmem] * 6,
        out_specs=vmem,
        out_shape=jax.ShapeDtypeStruct((tile_rows, 8, rows), jnp.float32),
        scratch_shapes=[
            pltpu.VMEM((rows, width), jnp.bfloat16),
            pltpu.VMEM((rows, width), jnp.bfloat16),
            pltpu.VMEM((padded, width), jnp.bfloat16),
            pltpu.VMEM((padded, width), jnp.bfloat16),
            pltpu.VMEM((6, rows, width), jnp.bfloat16),
            pltpu.VMEM((2, 3, rows, 128), jnp.float32),
            pltpu.VMEM((2, 8, rows), jnp.float32),
            pltpu.VMEM((8, rows), jnp.float32),
            pltpu.SemaphoreType.DMA((2, copies)),
        ],
        compiler_params=pltpu.CompilerParams(
            collective_id=1, has_side_effects=True, vmem_limit_bytes=48 << 20
        ),
    )(
        near[jnp.array([0, 2])][:, :, None],
        near[:, None, :],
        unit,
        spread,
        route,
        settle,
    )


def placing(target, count):
    return (jnp.arange(count, dtype=jnp.int32)[:, None] == target[None, :]).astype(jnp.bfloat16)


def permute(matrix, part):
    return jnp.dot(matrix, part, preferred_element_type=jnp.float32).astype(jnp.bfloat16)


def exclusive(values, axis):
    return jnp.cumsum(values, axis=axis) - values


def per_device(embeddings, labels):
    shard_rows, feature_dim = embeddings.shape
    tile_rows = lax.axis_size("tr")
    columns = lax.axis_size("tc")
    me = lax.axis_index("tr")
    place = lax.axis_index("tc")
    clusters = tile_rows * GROUP_CLUSTERS
    share = shard_rows // tile_rows
    capacity = -(-(share + tile_rows - 1) // 16) * 16
    i32 = jnp.int32

    onehot = labels[:, None] == jnp.arange(clusters, dtype=i32)[None, :]
    held = jnp.sum(onehot.astype(i32), axis=0)
    column, everywhere = gather_counts(held, tile_rows, columns)

    index = jnp.arange(shard_rows, dtype=i32)
    lower = (index[:, None] > index[None, :]).astype(jnp.bfloat16)
    ahead = jnp.dot(lower, onehot.astype(jnp.bfloat16), preferred_element_type=jnp.float32)
    rank = jnp.sum(jnp.where(onehot, ahead, 0.0), axis=1).astype(i32)
    starts = exclusive(held, 0)
    order = jnp.sum(jnp.where(onehot, starts[None, :], 0), axis=1) + rank

    values = embeddings.astype(jnp.float32)
    unit = (values * lax.rsqrt(jnp.sum(values * values, axis=1, keepdims=True) + EPSILON)).astype(
        jnp.bfloat16
    )

    def exchange(part, count):
        return lax.all_to_all(
            part.reshape(tile_rows, count, feature_dim),
            "tr",
            split_axis=0,
            concat_axis=0,
            tiled=True,
        ).reshape(tile_rows * count, feature_dim)

    spread = placing(order % tile_rows * share + order // tile_rows, shard_rows)

    local = exclusive(column, 1)
    group_count = column.reshape(tile_rows, tile_rows, GROUP_CLUSTERS).sum(2)
    group_start = exclusive(group_count, 1)
    via = jnp.arange(tile_rows, dtype=i32)

    def before(limit):
        return (limit[..., None] - via + tile_rows - 1) // tile_rows

    first = before(group_start)
    passed = before(group_start + group_count) - first
    base = exclusive(passed, 0) - first

    number = jnp.arange(share, dtype=i32)[None, :] * tile_rows + me
    inside = (number[:, :, None] >= group_start[:, None, :]) & (
        number[:, :, None] < (group_start + group_count)[:, None, :]
    )
    my_base = lax.dynamic_index_in_dim(base, me, 2, keepdims=False)
    lane = my_base[:, None, :] + number[:, :, None] // tile_rows
    target = jnp.sum(jnp.where(inside, via * capacity + lane, 0), axis=2).reshape(-1)
    route = placing(target, tile_rows * capacity)

    mine = lax.dynamic_slice_in_dim(column, me * GROUP_CLUSTERS, GROUP_CLUSTERS, 1)
    lengths = mine.T.reshape(-1)
    seg_start = exclusive(lengths, 0)
    seg_local = lax.dynamic_slice_in_dim(local, me * GROUP_CLUSTERS, GROUP_CLUSTERS, 1).T.reshape(-1)
    within = (index[:, None] >= seg_start[None, :]) & (
        index[:, None] < (seg_start + lengths)[None, :]
    )
    number = index + jnp.sum(jnp.where(within, (seg_local - seg_start)[None, :], 0), axis=1)
    way = number % tile_rows
    tables = lax.dynamic_index_in_dim(base, me, 1, keepdims=False)
    tables = jnp.tile(tables, (GROUP_CLUSTERS, 1))
    picked = jnp.sum(jnp.where(within[:, :, None], tables[None], 0), axis=1)
    offset = jnp.sum(jnp.where(way[:, None] == via[None, :], picked, 0), axis=1)
    source = way * capacity + offset + number // tile_rows
    settle = (
        source[:, None] == jnp.arange(tile_rows * capacity, dtype=i32)[None, :]
    ).astype(jnp.bfloat16)

    totals = lax.dynamic_slice_in_dim(everywhere, me * GROUP_CLUSTERS, GROUP_CLUSTERS, 1)
    ends = jnp.cumsum(totals, axis=1)[:, : GROUP_CLUSTERS - 1]
    key_labels = jnp.sum((index[None, :, None] >= ends[:, None, :]).astype(i32), axis=2)

    if columns == 8:
        back = plane_stats(unit, spread, route, settle, key_labels, place, tile_rows)
        back = jnp.stack([back[:, 0].reshape(-1), back[:, 1].reshape(-1)])
    else:
        landed = exchange(permute(spread, unit), share)
        arrived = exchange(permute(route, landed), capacity)
        queries = permute(settle, arrived)
        keys = lax.all_gather(queries, "tc", axis=0, tiled=True)
        query_labels = lax.dynamic_index_in_dim(key_labels, place, 0, keepdims=False)
        best, weighted = cluster_stats([queries], [keys], query_labels, key_labels.reshape(-1), place)
        back = lax.all_gather(jnp.stack([best, weighted]), "tr", axis=1, tiled=True)
    shard_before = exclusive(column, 0)
    begin = exclusive(column.sum(0), 0) + lax.dynamic_index_in_dim(
        shard_before, me, 0, keepdims=False
    )
    position = jnp.sum(jnp.where(onehot, begin[None, :], 0), axis=1) + rank
    here = position[:, None] == jnp.arange(tile_rows * shard_rows, dtype=i32)[None, :]
    best_sim = jnp.sum(jnp.where(here, back[0][None, :], 0.0), axis=1)
    mean_sim = jnp.sum(jnp.where(here, back[1][None, :], 0.0), axis=1)
    flag = jax.nn.sigmoid(SHARPNESS * (best_sim - THRESHOLD))
    return (best_sim, mean_sim, flag)


def solution(mesh):
    placed = (P(("tr", "tc"), None), P(("tr", "tc")))
    return jax.shard_map(
        per_device,
        mesh=mesh,
        in_specs=placed,
        out_specs=(P(("tr", "tc")), P(("tr", "tc")), P(("tr", "tc"))),
        check_vma=False,
    )
```
